128 devices in a mesh: role: 2 (over core), dev: 64 (over y, x, z).
Axes of the slice: x: 4, y: 4, z: 4, core: 2. Of those that a mesh axis runs over, the one named last changes fastest.
Arguments:
- queries: bfloat16 [2048, 32, 128], P('dev', 'role'), may hold values from -8 to 8
- keys_cache: bfloat16 [2048, 2, 192, 128], P('dev', 'role'), may hold values from -4 to 4
- values_cache: bfloat16 [2048, 2, 192, 128], P('dev', 'role'), may hold values from -4 to 4
- new_keys: bfloat16 [2048, 2, 128], P('dev', 'role'), may hold values from -4 to 4
- new_values: bfloat16 [2048, 2, 128], P('dev', 'role'), may hold values from -4 to 4
- lengths: int32 [2048], P('dev'), may hold values from 2 to 192, as said below
- norm_gain: float32 [4096], replicated, may hold values from 0.5 to 1.5
- expert_ids: int32 [2048, 8], P('dev'), may hold values from 0 to 127, all different within a row; in each aligned block of 16 rows (0 to 15, 16 to 31, ...) at most 2 rows name the same one
- route_weights: float32 [2048, 8], P('dev'), may hold values from 0.05 to 1
- gate_weight: bfloat16 [128, 4096, 768], P(('role', 'dev')), may hold values from -0.09375 to 0.09375
- up_weight: bfloat16 [128, 4096, 768], P(('role', 'dev')), may hold values from -0.09375 to 0.09375
- down_weight: bfloat16 [128, 768, 4096], P(('role', 'dev')), may hold values from -0.21875 to 0.21875
Outputs:
- mixed: bfloat16 [64, 2, 16, 4096], P('dev', 'role')
The draws below stay inside these ranges and needn't reach their ends.
Inputs may be any that keep to these rules, and one draw needn't show every extreme that they name: `lengths`: request 0's cache is full. `expert_ids`: in each aligned block of 16 rows (the tokens that one device routes) no expert is named by more than 2 rows.
All inputs are finite; a program needn't handle non-finite values.
Results may differ from the reference program's by a relative error of at most 0.013.
Values may be sent and summed in bfloat16 or wider, within the bound.
A program may use at most 128 MiB of HBM per device.

```python
import math
import jax
import jax.numpy as jnp
import numpy as np
from jax import lax

D = 4096
HEAD = 128
QH = 32
KV = 2
EXP_FF = 768
TOP = 8
TOK_DEV = 16
L = 192
EXPERTS = 128
CAP = 2
REQS = 2048
N_ROLE = 2


def draw_keys_cache(key, part):
    key = jax.random.fold_in(key, 17)
    keys = jnp.clip(jax.random.normal(key, (REQS, KV, L, HEAD), jnp.float32), -4.0, 4.0)
    return keys.astype(jnp.bfloat16)


def draw_queries(key, part):
    key = jax.random.fold_in(key, 23)
    queries = jnp.clip(jax.random.normal(key, (REQS, QH, HEAD), jnp.float32), -4.0, 4.0)
    return queries.astype(jnp.bfloat16)


def draw_lengths(key, part):
    key = jax.random.fold_in(key, 5)
    lengths = jax.random.randint(key, (REQS,), 2, L + 1).astype(jnp.int32)
    return lengths.at[0].set(L)


def block_scale(stream_key, extent, cuts, low, largest):
    def one(dim, blocks):
        draws = jax.random.uniform(jax.random.fold_in(jax.random.fold_in(stream_key, 6), dim), (blocks,), jnp.float32, low / len(cuts), largest / len(cuts))
        return jnp.repeat(jnp.exp(draws), extent[dim] // blocks).reshape((-1,) + (1,) * (len(extent) - dim - 1))

    factor_of = one(*cuts[0])
    for cut in cuts[1:]:
        factor_of = factor_of * one(*cut)
    return factor_of


def routed_block(key, own, number, rows, count, top, reach, slope):
    ranking = jax.random.permutation(key, count)
    packed, ordinary = load_shares(count, rows * top, reach, slope, True), load_shares(count, rows * top, reach, slope, False)
    places = jnp.arange(count)

    def named(sizes, offset_by):
        used = int((sizes > 0).sum())
        fixed = max(1, used // 4)
        moved = fixed + (places - fixed + offset_by * (used - fixed)) % max(1, count - fixed)
        return jnp.zeros((count,), jnp.int32).at[ranking[jnp.where(places < fixed, places, moved)]].set(jnp.asarray(sizes, jnp.int32))

    sizes = jnp.where(number % 4 == 0, named(packed, number // 4), named(ordinary, number - number // 4 - 1))
    mixed = jax.random.permutation(jax.random.fold_in(own, 3), count)
    giver, sink = mixed[0:count // 2 * 2:2], mixed[1:count // 2 * 2:2]
    margin = jnp.minimum(sizes[giver] - 1, reach - sizes[sink]) // 2
    margin = jnp.where((giver == ranking[0]) | (sink == ranking[0]) | (sizes[sink] == 0), 0, jnp.maximum(margin, 0))
    moved = jax.random.randint(jax.random.fold_in(own, 4), (count // 2,), 0, 1 << 20) % (margin + 1)
    sizes = sizes.at[giver].add(-moved).at[sink].add(moved)
    labels = jnp.searchsorted(jnp.cumsum(sizes), jnp.arange(rows * top), side="right").astype(jnp.int32)
    listing = labels.reshape(top, rows).T
    listing = listing[jax.random.permutation(jax.random.fold_in(own, 1), rows)]
    offset_by = jax.random.randint(jax.random.fold_in(own, 2), (rows, 1), 0, top)
    return jnp.take_along_axis(listing, (jnp.arange(top)[None, :] + offset_by) % top, axis=1)


def load_shares(amount, total, reach, slope, full):
    portions = [(1 << 20) // math.isqrt(grade ** slope) + 1 for grade in range(1, amount + 1)]
    largest = reach if full else min(reach, max(-(-total // amount), total * portions[0] // sum(portions)))
    least = 1 if total - largest >= amount - 1 else 0
    given, spare = [largest] + [least] * (amount - 1), total - largest - least * (amount - 1)
    while spare > 0:
        candidates = [i for i in range(1, amount) if given[i] < largest] or [i for i in range(1, amount) if given[i] < reach]
        mass, left = sum([portions[i] for i in candidates]), spare
        for i in candidates:
            more = min(reach - given[i], max(1, left * portions[i] // mass), spare)
            given[i] = given[i] + more
            spare = spare - more
    return np.array(given)


def bell_draw(stream_key, dims, width, reach, pieces=(), kind=jnp.bfloat16):
    loudness = block_scale(stream_key, dims, pieces, -0.22, 0.18) if pieces else 1.0
    values = jax.random.normal(stream_key, dims, jnp.float32) * width * loudness
    return jnp.minimum(jnp.maximum(values, -reach), reach).astype(kind)


def setup_inputs(seed: int = 0) -> dict:
    streams_of = jax.random.split(jax.random.key(seed), 13)
    queries = draw_queries(jax.random.fold_in(streams_of[12], 71), 0)
    keys_cache = draw_keys_cache(jax.random.fold_in(streams_of[12], 71), 0)
    values_cache = bell_draw(streams_of[2], (REQS, KV, L, HEAD), 1.0, 4.0, ((0, 64), (1, 2)))
    new_keys = bell_draw(streams_of[3], (REQS, KV, HEAD), 1.0, 4.0, ((0, 64), (1, 2)))
    new_values = bell_draw(streams_of[4], (REQS, KV, HEAD), 1.0, 4.0, ((0, 64), (1, 2)))
    lengths = draw_lengths(jax.random.fold_in(streams_of[12], 71), 0)
    norm_gain = jnp.clip(1.0 + 0.1 * jax.random.normal(streams_of[6], (D,), jnp.float32), 0.5, 1.5)
    expert_ids_keys = jax.random.split(jax.random.fold_in(streams_of[7], 1), REQS // TOK_DEV)
    expert_ids_turns = jax.random.permutation(jax.random.fold_in(streams_of[7], 3), REQS // TOK_DEV)
    expert_ids = jax.vmap(lambda own, number: routed_block(jax.random.fold_in(streams_of[7], 2), own, number, TOK_DEV, EXPERTS, TOP, CAP, 2))(expert_ids_keys, expert_ids_turns).reshape((REQS, TOP))
    route_weights = jnp.clip(jnp.exp(math.log(1.0) - 2.9957323 * jax.random.uniform(streams_of[8], (REQS, TOP), jnp.float32) ** block_scale(streams_of[8], (REQS, TOP), ((0, 64),), -0.2, 0.2)), 0.05, 1.0)
    gate_weight = bell_draw(streams_of[9], (EXPERTS, D, EXP_FF), D ** -0.5, 0.09375, ((0, 128),))
    up_weight = bell_draw(streams_of[10], (EXPERTS, D, EXP_FF), D ** -0.5, 0.09375, ((0, 128),))
    down_weight = bell_draw(streams_of[11], (EXPERTS, EXP_FF, D), EXP_FF ** -0.5, 0.21875, ((0, 128),))
    return {"queries": queries, "keys_cache": keys_cache, "values_cache": values_cache, "new_keys": new_keys, "new_values": new_values, "lengths": lengths, "norm_gain": norm_gain, "expert_ids": expert_ids, "route_weights": route_weights, "gate_weight": gate_weight, "up_weight": up_weight, "down_weight": down_weight}


def attend_block(queries, keys_cache, values_cache, new_keys, new_values, lengths):
    group = QH // KV
    rows = queries.shape[0]
    scale = HEAD ** (-0.5)
    query = queries.astype(jnp.float32).reshape(rows, KV, group, HEAD)
    scores = jnp.einsum('rkgd,rkld->rkgl', query, keys_cache.astype(jnp.float32)) * scale
    valid = jnp.arange(L, dtype=jnp.int32)[None, None, None, :] < lengths.astype(jnp.int32)[:, None, None, None]
    scores = jnp.where(valid, scores, -jnp.inf)
    own = jnp.einsum('rkgd,rkd->rkg', query, new_keys.astype(jnp.float32)) * scale
    peak = jnp.maximum(lax.optimization_barrier(jnp.max(scores, axis=-1)), own)
    weights = jnp.exp(scores - peak[..., None])
    own_weight = jnp.exp(own - peak)
    total = lax.optimization_barrier(jnp.sum(weights, axis=-1)) + own_weight
    probs = (weights / total[..., None]).astype(jnp.bfloat16)
    own_prob = (own_weight / total).astype(jnp.bfloat16)
    result = jnp.einsum('rkgl,rkld->rkgd', probs.astype(jnp.float32), values_cache.astype(jnp.float32))
    result = result + own_prob.astype(jnp.float32)[..., None] * new_values.astype(jnp.float32)[:, :, None, :]
    return result.reshape(rows, QH * HEAD).astype(jnp.bfloat16)

def expert_rows(rows, w_gate, w_up, w_down):
    gate = jnp.dot(rows, w_gate, preferred_element_type=jnp.float32)
    up_part = jnp.dot(rows, w_up, preferred_element_type=jnp.float32)
    hidden = (jax.nn.silu(gate) * up_part).astype(jnp.bfloat16)
    return jnp.dot(hidden, w_down, preferred_element_type=jnp.float32)

def reference(queries, keys_cache, values_cache, new_keys, new_values, lengths, norm_gain, expert_ids, route_weights, gate_weight, up_weight, down_weight):
    block = 64
    blocks = REQS // block

    def split(arr):
        return arr.reshape((blocks, block) + arr.shape[1:])
    attended = lax.map(lambda xs: attend_block(*xs), (split(queries), split(keys_cache), split(values_cache), split(new_keys), split(new_values), split(lengths)))
    attended = attended.reshape(REQS, D)
    wide = attended.astype(jnp.float32)
    normed = (wide * lax.rsqrt(lax.optimization_barrier(jnp.mean(wide * wide, axis=-1, keepdims=True)) + 1e-06) * norm_gain.astype(jnp.float32)).astype(jnp.bfloat16)
    share = route_weights / lax.optimization_barrier(jnp.sum(route_weights, axis=-1, keepdims=True))
    share_flat = share.reshape(-1)
    ids_flat = expert_ids.reshape(-1).astype(jnp.int32)
    order = jnp.argsort(ids_flat, stable=True).astype(jnp.int32)
    counts = lax.optimization_barrier(jnp.sum((ids_flat[None, :] == jnp.arange(EXPERTS, dtype=jnp.int32)[:, None]).astype(jnp.int32), axis=1))
    starts = (jnp.cumsum(counts) - counts).astype(jnp.int32)
    most = EXPERTS * CAP
    padded_order = jnp.concatenate([order, jnp.zeros((most,), jnp.int32)])

    def step(total, xs):
        w_gate, w_up, w_down, index = xs
        picked = lax.dynamic_slice_in_dim(padded_order, starts[index].astype(jnp.int32), most)
        live = jnp.arange(most, dtype=jnp.int32) < counts[index]
        route = jnp.where(live, picked, 0)
        token = route // TOP
        out = expert_rows(normed[token], w_gate, w_up, w_down)
        rounded = lax.optimization_barrier(out.astype(jnp.bfloat16))
        term = rounded.astype(jnp.float32) * share_flat[route][:, None]
        target = jnp.where(live, token, REQS)
        return (total.at[target].add(term, mode='drop'), None)
    moe, unused = lax.scan(step, jnp.zeros((REQS, D), jnp.float32), (gate_weight, up_weight, down_weight, jnp.arange(EXPERTS, dtype=jnp.int32)))
    mixed = (attended.astype(jnp.float32) + moe).astype(jnp.bfloat16)
    return mixed.reshape(REQS // (N_ROLE * TOK_DEV), N_ROLE, TOK_DEV, D)
```

```python
import jax
import jax.numpy as jnp
from jax import lax
from jax.experimental import pallas as pl
from jax.experimental.pallas import tpu as pltpu
from jax.sharding import PartitionSpec as P

HEAD = 128
HEADS = 16
TOK = 32
LEN = 192
LEN_PAD = 208
HALF = 2048
WIDTH = 4096
FF = 768
EXPERTS = 128
STRIDES = (16, 4, 1)
ORDERS = ((1, 0, 2), (0, 2, 1), (2, 1, 0))
CHUNKS = ((384, 384, 256), (384, 256, 384))
PIECES = []
for _j, _sizes in enumerate(CHUNKS):
    _at = _j * 1024
    for _k, _size in enumerate(_sizes):
        PIECES.append((_j, _k, _at, _size))
        _at += _size
N = len(PIECES)
MESH = pl.DeviceIdType.MESH
BF = jnp.bfloat16
F32 = jnp.float32


def rows_dot(a, b):
    return lax.dot_general(a, b, (((1,), (1,)), ((), ())), preferred_element_type=F32)


def dot(a, b):
    return jnp.dot(a, b, preferred_element_type=F32)


def kernel(
    lengths,
    ids,
    route,
    gain,
    queries,
    new_keys,
    new_values,
    keys_hbm,
    values_hbm,
    gate_hbm,
    up_hbm,
    down_hbm,
    out,
    *scratch,
):
    refs = list(scratch)

    def take(count):
        taken = refs[:count]
        del refs[:count]
        return taken

    gathered, picked, arrived, produced, returned, partial, parts, summed, pieces = (
        take(N) for _ in range(9)
    )
    meta = take(3)
    (keys, values, heads, gate_w, up_w, down_w, normed, gate, up, hidden, squares) = take(11)
    select, combine, other, mixed = take(4)
    (load_sem, weight_sem, meta_sem, g1_sem, g2_sem, ex_sem, back_sem, r1_sem, r2_sem, swap_sem) = (
        take(10)
    )

    role = lax.axis_index("role")
    dev = lax.axis_index("dev")
    here = (dev // 16, (dev // 4) % 4, dev % 4)

    def at(axis, value):
        return dev + (value - here[axis]) * STRIDES[axis]

    def along(axis, step):
        return lax.rem(here[axis] + step, 4)

    def send(src, dst, sems, index, target):
        pltpu.make_async_remote_copy(
            src_ref=src,
            dst_ref=dst,
            send_sem=sems.at[0, index],
            recv_sem=sems.at[1, index],
            device_id=target,
            device_id_type=MESH,
        ).start()

    def settle(ref, sem):
        pltpu.make_async_copy(ref, ref, sem).wait()

    loads = []
    for part in range(2):
        span = pl.ds(part * 16, 16)
        for n, (src, dst) in enumerate(((keys_hbm, keys), (values_hbm, values))):
            copy = pltpu.make_async_copy(
                src.at[span, 0], dst.at[span, pl.ds(0, LEN)], load_sem.at[part, n]
            )
            copy.start()
            loads.append(copy)
    weights = []
    for n, (src, dst) in enumerate(((gate_hbm, gate_w), (up_hbm, up_w), (down_hbm, down_w))):
        copy = pltpu.make_async_copy(src.at[0], dst, weight_sem.at[n])
        copy.start()
        weights.append(copy)

    barrier = pltpu.get_barrier_semaphore()
    for axis in range(3):
        for step in (1, 2, 3):
            for who in range(2):
                pl.semaphore_signal(
                    barrier, inc=1, device_id=(who, at(axis, along(axis, step))), device_id_type=MESH
                )
    pl.semaphore_signal(barrier, inc=1, device_id=(1 - role, dev), device_id_type=MESH)

    lane = lax.broadcasted_iota(jnp.int32, (TOK, EXPERTS), 1)
    share = route[...] / jnp.sum(route[...], axis=1, keepdims=True)
    named = ids[...]
    hit = jnp.zeros((TOK, EXPERTS), F32)
    shares = jnp.zeros((TOK, EXPERTS), F32)
    for k in range(named.shape[1]):
        same = named[:, k : k + 1] == lane
        hit = jnp.where(same, 1.0, hit)
        shares = jnp.where(same, share[:, k : k + 1], shares)
    row = lax.broadcasted_iota(jnp.int32, (TOK, TOK), 0)
    col = lax.broadcasted_iota(jnp.int32, (TOK, TOK), 1)
    before = jnp.where((row // 16 == col // 16) & (col < row), 1.0, 0.0).astype(BF)
    second = dot(before, hit.astype(BF))
    signed = jnp.where(second > 0.5, -shares, shares).astype(BF)
    for k, (a1, a2, _) in enumerate(ORDERS):
        meta[k][here[a2], here[a1]] = signed

    scale = HEAD ** (-0.5)
    first_row = lax.broadcasted_iota(jnp.int32, (16, HEAD), 0) == 0
    place = lax.broadcasted_iota(jnp.int32, (HEADS, LEN_PAD), 1)

    def attend(first):
        probs = []
        for n in range(8):
            r = first + n
            own_key = jnp.broadcast_to(new_keys[r], (16, HEAD)).astype(F32)
            own_value = jnp.broadcast_to(new_values[r], (16, HEAD)).astype(F32)
            keys[r, LEN:LEN_PAD, :] = jnp.where(first_row, own_key, 0.0).astype(BF)
            values[r, LEN:LEN_PAD, :] = jnp.where(first_row, own_value, 0.0).astype(BF)
            scores = rows_dot(queries[r], keys[r]) * scale
            live = (place < lengths[r]) | (place == LEN)
            probs.append(jnp.where(live, scores, -jnp.inf))
        scores = jnp.concatenate(probs, axis=0)
        spread = jnp.exp(scores - jnp.max(scores, axis=1, keepdims=True))
        spread = (spread / jnp.sum(spread, axis=1, keepdims=True)).astype(BF)
        for n in range(8):
            r = first + n
            start = pl.multiple_of(r * HEADS, HEADS)
            heads[pl.ds(start, HEADS), :] = dot(spread[n * HEADS : (n + 1) * HEADS], values[r])

    def attend_half(part):
        def step(n, carry):
            attend(part * 16 + n * 8)
            return carry

        loads[2 * part].wait()
        loads[2 * part + 1].wait()
        lax.fori_loop(0, 2, step, 0)

    attend_half(0)
    pl.semaphore_wait(barrier, 19)
    for k, (a1, a2, _) in enumerate(ORDERS):
        for step in (2, 1, 3):
            block = meta[k].at[here[a2], here[a1]]
            send(block, block, meta_sem, k, (role, at(a1, along(a1, step))))
    attend_half(1)

    for i, (_, k, first, size) in enumerate(PIECES):
        a1, a2, _ = ORDERS[k]
        for h in range(size // HEAD):
            head = first // HEAD + h
            gathered[i][here[a2], here[a1], :, h * HEAD : (h + 1) * HEAD] = heads[
                pl.ds(head, TOK, stride=HEADS), :
            ].astype(BF)
        for step in (2, 1, 3):
            block = gathered[i].at[here[a2], here[a1]]
            send(block, block, g1_sem, i, (role, at(a1, along(a1, step))))

    for k, (a1, a2, _) in enumerate(ORDERS):
        settle(meta[k].at[0, pl.ds(0, 3)], meta_sem.at[1, k])
        for step in (2, 1, 3):
            block = meta[k].at[here[a2]]
            send(block, block, meta_sem, 3 + k, (role, at(a2, along(a2, step))))

    for i, (_, k, _, _) in enumerate(PIECES):
        a1, a2, _ = ORDERS[k]
        settle(gathered[i].at[0, pl.ds(0, 3)], g1_sem.at[1, i])
        for step in (2, 1, 3):
            block = gathered[i].at[here[a2]]
            send(block, block, g2_sem, i, (role, at(a2, along(a2, step))))

    row = lax.broadcasted_iota(jnp.int32, (128, 128), 0)
    col = lax.broadcasted_iota(jnp.int32, (128, 128), 1)
    for k, (_, _, a3) in enumerate(ORDERS):
        settle(meta[k].at[pl.ds(0, 3)], meta_sem.at[1, 3 + k])
        expert = ((row // 16) % 2) * 64 + at(a3, row // 32)
        chosen = jnp.where(expert == col, 1.0, 0.0).astype(BF)
        for b in range(4):
            marks = meta[k][b].reshape(128, EXPERTS)
            wide = rows_dot(chosen, marks)
            wide = jnp.where(row % 2 == 0, wide, -wide)
            mask = ((row % 16) // 2 == col // 16) & (wide > 0.0)
            select[k, b] = jnp.where(mask, 1.0, 0.0).astype(BF)
            tall = rows_dot(marks, chosen)
            tall = jnp.where(col % 2 == 0, tall, -tall)
            mask = ((col % 16) // 2 == row // 16) & (tall > 0.0)
            combine[k, b] = jnp.where(mask, tall, 0.0).astype(BF)

    for i, (_, k, _, size) in enumerate(PIECES):
        a3 = ORDERS[k][2]
        settle(gathered[i].at[pl.ds(0, 3)], g2_sem.at[1, i])
        for b in range(4):
            rows = dot(select[k, b], gathered[i][b].reshape(128, size)).astype(BF)
            picked[i][:, b * 16 : (b + 1) * 16, :] = rows.reshape(8, 16, size)
        for step in (2, 1, 3):
            there = along(a3, step)
            for who in range(2):
                send(
                    picked[i].at[there * 2 + who],
                    arrived[i].at[role, here[a3]],
                    ex_sem,
                    i,
                    (who, at(a3, there)),
                )
        send(
            picked[i].at[here[a3] * 2 + 1 - role],
            arrived[i].at[role, here[a3]],
            ex_sem,
            i,
            (1 - role, dev),
        )
        pltpu.make_async_copy(
            picked[i].at[here[a3] * 2 + role], arrived[i].at[role, here[a3]], ex_sem.at[1, i]
        ).start()

    row = lax.broadcasted_iota(jnp.int32, (256, 256), 0)
    col = lax.broadcasted_iota(jnp.int32, (256, 256), 1)

    def common(index):
        a1, a2, a3 = ORDERS[0]
        place = {a3: index // 64, a2: (index // 16) % 4, a1: (index // 4) % 4}
        return place

    def turned(index, k):
        place = common(index)
        a1, a2, a3 = ORDERS[k]
        return place[a3] * 64 + place[a2] * 16 + place[a1] * 4 + index % 4

    squares[...] = jnp.zeros_like(squares)
    gate[...] = jnp.zeros_like(gate)
    up[...] = jnp.zeros_like(up)
    weights[0].wait()
    weights[1].wait()
    for j in range(len(CHUNKS)):
        for i, (chunk, k, first, size) in enumerate(PIECES):
            if chunk != j:
                continue
            settle(arrived[i], ex_sem.at[1, i])
            for c in range(2):
                rows = arrived[i][c].reshape(256, size)
                if k == 0:
                    rows = rows.astype(F32)
                else:
                    rows = dot(jnp.where(turned(row, k) == col, 1.0, 0.0).astype(BF), rows)
                begin = c * HALF + first
                total = squares[...]
                for t in range(size // HEAD):
                    tile = rows[:, t * HEAD : (t + 1) * HEAD]
                    total = total + tile * tile
                squares[...] = total
                normed[:, begin : begin + size] = (rows * gain[:, begin : begin + size]).astype(BF)
        for c in range(2):
            begin = c * HALF + j * 1024

            def tile(n, carry, begin=begin):
                cols = pl.ds(pl.multiple_of(n * 256, 256), 256)
                left = normed[:, begin : begin + 1024]
                gate[:, cols] += dot(left, gate_w[begin : begin + 1024, cols])
                up[:, cols] += dot(left, up_w[begin : begin + 1024, cols])
                return carry

            lax.fori_loop(0, FF // 256, tile, 0)

    factor = lax.rsqrt(jnp.sum(squares[...], axis=1, keepdims=True) * (1.0 / WIDTH) + 1e-06)
    gated = gate[...] * factor
    hidden[0] = (gated / (1.0 + jnp.exp(-gated)) * (up[...] * factor)).astype(BF)
    for k in (1, 2):
        turn = jnp.where(turned(col, k) == row, 1.0, 0.0).astype(BF)
        hidden[k] = dot(turn, hidden[0]).astype(BF)

    weights[2].wait()
    for i, (_, k, first, size) in enumerate(PIECES):
        a3 = ORDERS[k][2]
        for c in range(2):
            begin = c * HALF + first
            rows = dot(hidden[k], down_w[:, begin : begin + size]).astype(BF)
            produced[i][c] = rows.reshape(4, 64, size)
        for step in (2, 1, 3):
            there = along(a3, step)
            for who in range(2):
                send(
                    produced[i].at[who, there],
                    returned[i].at[here[a3] * 2 + role],
                    back_sem,
                    i,
                    (who, at(a3, there)),
                )
        send(
            produced[i].at[1 - role, here[a3]],
            returned[i].at[here[a3] * 2 + role],
            back_sem,
            i,
            (1 - role, dev),
        )
        pltpu.make_async_copy(
            produced[i].at[role, here[a3]],
            returned[i].at[here[a3] * 2 + role],
            back_sem.at[1, i],
        ).start()

    for i, (_, k, _, size) in enumerate(PIECES):
        a2 = ORDERS[k][1]
        settle(returned[i], back_sem.at[1, i])
        for b in range(4):
            rows = returned[i][:, b * 16 : (b + 1) * 16, :].reshape(128, size)
            partial[i][b] = dot(combine[k, b], rows).astype(BF)
        for step in (2, 1, 3):
            there = along(a2, step)
            send(
                partial[i].at[there], parts[i].at[here[a2]], r1_sem, i, (role, at(a2, there))
            )
        pltpu.make_async_copy(
            partial[i].at[here[a2]], parts[i].at[here[a2]], r1_sem.at[1, i]
        ).start()

    for i, (_, k, _, size) in enumerate(PIECES):
        a1 = ORDERS[k][0]
        settle(parts[i], r1_sem.at[1, i])
        total = parts[i][0].astype(F32)
        for b in range(1, 4):
            total = total + parts[i][b].astype(F32)
        summed[i][...] = total.astype(BF).reshape(4, TOK, size)
        for step in (2, 1, 3):
            there = along(a1, step)
            send(
                summed[i].at[there], pieces[i].at[here[a1]], r2_sem, i, (role, at(a1, there))
            )
        pltpu.make_async_copy(
            summed[i].at[here[a1]], pieces[i].at[here[a1]], r2_sem.at[1, i]
        ).start()

    for i, (_, k, first, size) in enumerate(PIECES):
        a1, a2, _ = ORDERS[k]
        settle(pieces[i], r2_sem.at[1, i])
        total = pieces[i][0].astype(F32)
        for b in range(1, 4):
            total = total + pieces[i][b].astype(F32)
        total = total + gathered[i][here[a2], here[a1]].astype(F32)
        mixed[:, :, first : first + size] = total.astype(BF).reshape(2, 16, size)
    swap = pltpu.make_async_remote_copy(
        src_ref=mixed.at[1 - role],
        dst_ref=other,
        send_sem=swap_sem.at[0],
        recv_sem=swap_sem.at[1],
        device_id=(1 - role, dev),
        device_id_type=MESH,
    )
    swap.start()
    out[:, pl.ds(pl.multiple_of(role * HALF, HALF), HALF)] = mixed[role]
    swap.wait()
    out[:, pl.ds(pl.multiple_of((1 - role) * HALF, HALF), HALF)] = other[...]

    for k in range(3):
        settle(meta[k].at[0, pl.ds(0, 3)], meta_sem.at[0, k])
        settle(meta[k].at[pl.ds(0, 3)], meta_sem.at[0, 3 + k])
    for i in range(N):
        settle(gathered[i].at[0, pl.ds(0, 3)], g1_sem.at[0, i])
        settle(gathered[i].at[pl.ds(0, 3)], g2_sem.at[0, i])
        settle(picked[i].at[pl.ds(0, 7)], ex_sem.at[0, i])
        settle(picked[i].at[pl.ds(0, 7)], back_sem.at[0, i])
        settle(partial[i].at[pl.ds(0, 3)], r1_sem.at[0, i])
        settle(summed[i].at[pl.ds(0, 3)], r2_sem.at[0, i])


def per_device(
    queries,
    keys_cache,
    values_cache,
    new_keys,
    new_values,
    lengths,
    norm_gain,
    expert_ids,
    route_weights,
    gate_weight,
    up_weight,
    down_weight,
):
    sizes = [size for _, _, _, size in PIECES]

    def buffers(*lead):
        return [pltpu.VMEM((*lead, size), BF) for size in sizes]

    vmem = pl.BlockSpec(memory_space=pltpu.VMEM)
    hbm = pl.BlockSpec(memory_space=pl.ANY)
    mixed = pl.pallas_call(
        kernel,
        name="layer",
        out_shape=jax.ShapeDtypeStruct((16, WIDTH), BF),
        in_specs=[pl.BlockSpec(memory_space=pltpu.SMEM)] + [vmem] * 6 + [hbm] * 5,
        out_specs=vmem,
        scratch_shapes=[
            *buffers(4, 4, TOK),
            *buffers(8, 64),
            *buffers(2, 4, 64),
            *buffers(2, 4, 64),
            *buffers(8, 64),
            *buffers(4, 128),
            *buffers(4, 128),
            *buffers(4, TOK),
            *buffers(4, TOK),
            *[pltpu.VMEM((4, 4, TOK, EXPERTS), BF)] * 3,
            pltpu.VMEM((TOK, LEN_PAD, HEAD), BF),
            pltpu.VMEM((TOK, LEN_PAD, HEAD), BF),
            pltpu.VMEM((TOK * HEADS, HEAD), F32),
            pltpu.VMEM((WIDTH, FF), BF),
            pltpu.VMEM((WIDTH, FF), BF),
            pltpu.VMEM((FF, WIDTH), BF),
            pltpu.VMEM((256, WIDTH), BF),
            pltpu.VMEM((256, FF), F32),
            pltpu.VMEM((256, FF), F32),
            pltpu.VMEM((3, 256, FF), BF),
            pltpu.VMEM((256, HEAD), F32),
            pltpu.VMEM((3, 4, 128, 128), BF),
            pltpu.VMEM((3, 4, 128, 128), BF),
            pltpu.VMEM((16, HALF), BF),
            pltpu.VMEM((2, 16, HALF), BF),
            pltpu.SemaphoreType.DMA((2, 2)),
            pltpu.SemaphoreType.DMA((3,)),
            pltpu.SemaphoreType.DMA((2, 6)),
            *[pltpu.SemaphoreType.DMA((2, N))] * 6,
            pltpu.SemaphoreType.DMA((2,)),
        ],
        compiler_params=pltpu.CompilerParams(
            collective_id=0, has_side_effects=True, vmem_limit_bytes=60 * 2**20
        ),
        cost_estimate=pl.CostEstimate(
            flops=6 * 256 * WIDTH * FF, bytes_accessed=22 * 2**20, transcendentals=0
        ),
    )(
        lengths,
        expert_ids,
        route_weights,
        norm_gain.reshape(1, WIDTH),
        queries,
        new_keys,
        new_values,
        keys_cache,
        values_cache,
        gate_weight,
        up_weight,
        down_weight,
    )
    return mixed.reshape(1, 1, 16, WIDTH)


def solution(mesh):
    return jax.shard_map(
        per_device,
        mesh=mesh,
        in_specs=(
            P("dev", "role", None),
            P("dev", "role", None, None),
            P("dev", "role", None, None),
            P("dev", "role", None),
            P("dev", "role", None),
            P("dev"),
            P(),
            P("dev", None),
            P("dev", None),
            P(("role", "dev"), None, None),
            P(("role", "dev"), None, None),
            P(("role", "dev"), None, None),
        ),
        out_specs=P("dev", "role", None, None),
        check_vma=False,
    )
```

```python
import jax
import jax.numpy as jnp
from jax import lax
from jax.experimental import pallas as pl
from jax.experimental.pallas import tpu as pltpu
from jax.sharding import PartitionSpec as P

HEAD = 128
HEADS = 16
TOK = 16
LEN = 192
LEN_PAD = 208
HALF = 2048
WIDTH = 4096
FF = 768
EXPERTS = 128
STRIDES = (16, 4, 1)
ORDERS = ((1, 0, 2), (0, 2, 1), (2, 1, 0))
SIZES = (768, 640, 640)
FIRSTS = (0, 768, 1408)
MESH = pl.DeviceIdType.MESH
VMEM_LIMIT = 56 * 2**20
BF = jnp.bfloat16
F32 = jnp.float32


def rows_dot(a, b):
    return lax.dot_general(a, b, (((1,), (1,)), ((), ())), preferred_element_type=F32)


def dot(a, b):
    return jnp.dot(a, b, preferred_element_type=F32)


def iotas(rows, cols):
    shape = (rows, cols)
    return lax.broadcasted_iota(jnp.int32, shape, 0), lax.broadcasted_iota(jnp.int32, shape, 1)


def kernel(
    lengths,
    ids,
    route,
    gain,
    queries,
    new_keys,
    new_values,
    keys_hbm,
    values_hbm,
    gate_hbm,
    up_hbm,
    down_hbm,
    out,
    *scratch,
):
    refs = list(scratch)

    def take(count):
        taken = refs[:count]
        del refs[:count]
        return taken

    gathered, picked, arrived, produced, returned, partial, parts, summed, pieces, resid, meta = (
        take(3) for _ in range(11)
    )
    (keys, values, heads, gate_w, up_w, down_w, normed, gate, up, hidden) = take(10)
    select, combine = take(2)
    (load_sem, weight_sem, meta_sem, g1_sem, g2_sem, ex_sem, back_sem, r1_sem, r2_sem, own_sem) = (
        take(10)
    )

    role = lax.axis_index("role")
    dev = lax.axis_index("dev")
    here = (dev // 16, (dev // 4) % 4, dev % 4)

    def at(axis, value):
        return dev + (value - here[axis]) * STRIDES[axis]

    def along(axis, step):
        return lax.rem(here[axis] + step, 4)

    def send(src, dst, send_sem, recv_sem, target):
        pltpu.make_async_remote_copy(
            src_ref=src,
            dst_ref=dst,
            send_sem=send_sem,
            recv_sem=recv_sem,
            device_id=target,
            device_id_type=MESH,
        ).start()

    def pair(sems, b, k):
        return sems.at[0, b, k], sems.at[1, b, k]

    def keep(src, dst, sems, b, k):
        pltpu.make_async_copy(src, dst, sems.at[1, b, k]).start()

    def settle(ref, sem):
        pltpu.make_async_copy(ref, ref, sem).wait()

    loads = []
    for b in range(2):
        span = pl.ds(b * TOK, TOK)
        for n, (src, dst) in enumerate(((keys_hbm, keys), (values_hbm, values))):
            copy = pltpu.make_async_copy(
                src.at[span, 0], dst.at[span, pl.ds(0, LEN)], load_sem.at[b, n]
            )
            copy.start()
            loads.append(copy)
    weights = [
        pltpu.make_async_copy(src.at[0], dst, weight_sem.at[n])
        for n, (src, dst) in enumerate(((gate_hbm, gate_w), (up_hbm, up_w), (down_hbm, down_w)))
    ]

    barrier = pltpu.get_barrier_semaphore()
    for axis in range(3):
        for step in (1, 2, 3):
            for who in range(2):
                pl.semaphore_signal(
                    barrier, inc=1, device_id=(who, at(axis, along(axis, step))), device_id_type=MESH
                )
    pl.semaphore_signal(barrier, inc=1, device_id=(1 - role, dev), device_id_type=MESH)

    both = 2 * TOK
    row, col = iotas(EXPERTS, both)
    share = route[...] / jnp.sum(route[...], axis=0, keepdims=True)
    named = ids[...]
    hit = jnp.zeros((EXPERTS, both), F32)
    shares = jnp.zeros((EXPERTS, both), F32)
    for k in range(named.shape[0]):
        same = named[k : k + 1, :] == row
        hit = jnp.where(same, 1.0, hit)
        shares = jnp.where(same, share[k : k + 1, :], shares)
    row, col = iotas(both, both)
    before = jnp.where((row // TOK == col // TOK) & (row < col), 1.0, 0.0).astype(BF)
    second = dot(hit.astype(BF), before)
    signed = jnp.where(second > 0.5, -shares, shares).astype(BF)
    signed = rows_dot(jnp.where(row == col, 1.0, 0.0).astype(BF), signed).astype(BF)
    for k, (a1, a2, _) in enumerate(ORDERS):
        meta[k][here[a2], here[a1]] = signed

    scale = HEAD ** (-0.5)
    first_row = lax.broadcasted_iota(jnp.int32, (16, HEAD), 0) == 0
    place = lax.broadcasted_iota(jnp.int32, (HEADS, LEN_PAD), 1)

    def attend(first):
        scores = []
        for n in range(8):
            r = first + n
            own_key = jnp.broadcast_to(new_keys[pl.ds(r, 1), :], (16, HEAD)).astype(F32)
            own_value = jnp.broadcast_to(new_values[pl.ds(r, 1), :], (16, HEAD)).astype(F32)
            keys[r, LEN:LEN_PAD, :] = jnp.where(first_row, own_key, 0.0).astype(BF)
            values[r, LEN:LEN_PAD, :] = jnp.where(first_row, own_value, 0.0).astype(BF)
            live = (place < lengths[r]) | (place == LEN)
            scores.append(jnp.where(live, rows_dot(queries[r], keys[r]) * scale, -jnp.inf))
        scores = jnp.concatenate(scores, axis=0)
        spread = jnp.exp(scores - jnp.max(scores, axis=1, keepdims=True))
        spread = (spread / jnp.sum(spread, axis=1, keepdims=True)).astype(BF)
        for n in range(8):
            r = first + n
            heads[r * HEADS : (r + 1) * HEADS, :] = dot(
                spread[n * HEADS : (n + 1) * HEADS], values[r]
            )

    def attend_batch(b):
        loads[2 * b].wait()
        loads[2 * b + 1].wait()
        for n in range(2):
            attend(b * TOK + n * 8)

    def put(b):
        for k, (a1, a2, _) in enumerate(ORDERS):
            block = gathered[k].at[b, here[a2], here[a1]]
            for h in range(SIZES[k] // HEAD):
                head = FIRSTS[k] // HEAD + h
                block[:, h * HEAD : (h + 1) * HEAD] = heads[
                    pl.ds(b * TOK * HEADS + head, TOK, stride=HEADS), :
                ].astype(BF)
            for step in (2, 1, 3):
                send(block, block, *pair(g1_sem, b, k), (role, at(a1, along(a1, step))))

    def relay(b):
        for k, (a1, a2, _) in enumerate(ORDERS):
            settle(gathered[k].at[b, 0, pl.ds(0, 3)], g1_sem.at[1, b, k])
            block = gathered[k].at[b, here[a2]]
            for step in (2, 1, 3):
                send(block, block, *pair(g2_sem, b, k), (role, at(a2, along(a2, step))))

    def tables(b):
        row, col = iotas(256, EXPERTS)
        tall_row, tall_col = iotas(256, 256)
        for k, (_, _, a3) in enumerate(ORDERS):
            expert = ((row // 32) % 2) * 64 + at(a3, row // 64)
            chosen = jnp.where(expert == col, 1.0, 0.0).astype(BF)
            marks = meta[k][:, :, b * TOK : (b + 1) * TOK, :].reshape(256, EXPERTS)
            wide = rows_dot(chosen, marks)
            wide = jnp.where(tall_row % 2 == 0, wide, -wide)
            mask = ((tall_row % 32) // 2 == tall_col // TOK) & (wide > 0.0)
            select[b, k] = jnp.where(mask, 1.0, 0.0).astype(BF)
            tall = rows_dot(marks, chosen)
            tall = jnp.where(tall_col % 2 == 0, tall, -tall)
            mask = ((tall_col % 32) // 2 == tall_row // TOK) & (tall > 0.0)
            combine[b, k] = jnp.where(mask, tall, 0.0).astype(BF)

    def pick(b):
        for k, (_, _, a3) in enumerate(ORDERS):
            settle(gathered[k].at[b, pl.ds(0, 3)], g2_sem.at[1, b, k])
            rows = dot(select[b, k], gathered[k][b].reshape(256, SIZES[k]))
            picked[k][b] = rows.astype(BF).reshape(8, 32, SIZES[k])
            there = arrived[k].at[b, role, here[a3]]
            for step in (2, 1, 3):
                z = along(a3, step)
                for who in range(2):
                    send(picked[k].at[b, z * 2 + who], there, *pair(ex_sem, b, k), (who, at(a3, z)))
            mine = here[a3] * 2
            send(picked[k].at[b, mine + 1 - role], there, *pair(ex_sem, b, k), (1 - role, dev))
            keep(picked[k].at[b, mine + role], there, ex_sem, b, k)

    def turned(index, k):
        a1, a2, a3 = ORDERS[0]
        place = {a3: index // 32, a2: (index // 8) % 4, a1: (index // 2) % 4}
        a1, a2, a3 = ORDERS[k]
        return place[a3] * 32 + place[a2] * 8 + place[a1] * 2 + index % 2

    def expert_in(b):
        squares = jnp.zeros((128, HEAD), F32)
        row, col = iotas(128, 128)
        for k in range(3):
            settle(arrived[k].at[b], ex_sem.at[1, b, k])
            for c in range(2):
                rows = arrived[k][b, c].reshape(128, SIZES[k])
                if k == 0:
                    rows = rows.astype(F32)
                else:
                    rows = dot(jnp.where(turned(row, k) == col, 1.0, 0.0).astype(BF), rows)
                for t in range(SIZES[k] // HEAD):
                    tile = rows[:, t * HEAD : (t + 1) * HEAD]
                    squares = squares + tile * tile
                begin = c * HALF + FIRSTS[k]
                normed[:, begin : begin + SIZES[k]] = (
                    rows * gain[:, begin : begin + SIZES[k]]
                ).astype(BF)
        if b == 0:
            weights[0].wait()
            weights[1].wait()

        def tile(n, carry):
            cols = pl.ds(pl.multiple_of(n * 256, 256), 256)
            gate[:, cols] = dot(normed[...], gate_w[:, cols])
            up[:, cols] = dot(normed[...], up_w[:, cols])
            return carry

        lax.fori_loop(0, FF // 256, tile, 0)
        factor = lax.rsqrt(jnp.sum(squares, axis=1, keepdims=True) * (1.0 / WIDTH) + 1e-06)
        gated = gate[...] * factor
        hidden[0] = (gated / (1.0 + jnp.exp(-gated)) * (up[...] * factor)).astype(BF)
        for k in (1, 2):
            turn = jnp.where(turned(col, k) == row, 1.0, 0.0).astype(BF)
            hidden[k] = dot(turn, hidden[0]).astype(BF)

    def expert_out(b):
        if b == 0:
            weights[2].wait()
        for k, (_, _, a3) in enumerate(ORDERS):
            for c in range(2):
                begin = c * HALF + FIRSTS[k]
                rows = dot(hidden[k], down_w[:, begin : begin + SIZES[k]])
                produced[k][b, c] = rows.astype(BF).reshape(4, 32, SIZES[k])
            there = returned[k].at[b, here[a3] * 2 + role]
            for step in (2, 1, 3):
                z = along(a3, step)
                for who in range(2):
                    send(produced[k].at[b, who, z], there, *pair(back_sem, b, k), (who, at(a3, z)))
            send(produced[k].at[b, 1 - role, here[a3]], there, *pair(back_sem, b, k), (1 - role, dev))
            keep(produced[k].at[b, role, here[a3]], there, back_sem, b, k)

    def merge(b):
        for k, (_, a2, _) in enumerate(ORDERS):
            settle(returned[k].at[b], back_sem.at[1, b, k])
            rows = dot(combine[b, k], returned[k][b].reshape(256, SIZES[k]))
            partial[k][b] = rows.astype(BF).reshape(4, 64, SIZES[k])
            there = parts[k].at[b, here[a2]]
            for step in (2, 1, 3):
                z = along(a2, step)
                send(partial[k].at[b, z], there, *pair(r1_sem, b, k), (role, at(a2, z)))
            keep(partial[k].at[b, here[a2]], there, r1_sem, b, k)

    def fold(b):
        for k, (a1, _, _) in enumerate(ORDERS):
            settle(parts[k].at[b], r1_sem.at[1, b, k])
            total = parts[k][b, 0].astype(F32)
            for n in range(1, 4):
                total = total + parts[k][b, n].astype(F32)
            summed[k][b] = total.astype(BF).reshape(4, TOK, SIZES[k])
            there = pieces[k].at[role, here[a1]]
            for step in (2, 1, 3):
                z = along(a1, step)
                send(summed[k].at[b, z], there, r2_sem.at[0, b, k], r2_sem.at[1, 0, k], (b, at(a1, z)))

            @pl.when(role == b)
            def _(k=k, a1=a1, there=there):
                keep(summed[k].at[b, here[a1]], there, r2_sem, 0, k)

            @pl.when(role != b)
            def _(k=k, a1=a1, there=there):
                send(
                    summed[k].at[b, here[a1]],
                    there,
                    own_sem.at[0, 1, k],
                    r2_sem.at[1, 0, k],
                    (b, dev),
                )

    pl.semaphore_wait(barrier, 19)
    for k, (a1, a2, _) in enumerate(ORDERS):
        block = meta[k].at[here[a2], here[a1]]
        for step in (2, 1, 3):
            send(block, block, *pair(meta_sem, 0, k), (role, at(a1, along(a1, step))))
    attend_batch(0)
    put(0)
    attend_batch(1)
    put(1)
    for copy in weights:
        copy.start()
    for k, (a1, a2, _) in enumerate(ORDERS):
        settle(meta[k].at[0, pl.ds(0, 3)], meta_sem.at[1, 0, k])
        block = meta[k].at[here[a2]]
        for step in (2, 1, 3):
            send(block, block, *pair(meta_sem, 1, k), (role, at(a2, along(a2, step))))
    relay(0)
    for k, (a1, a2, _) in enumerate(ORDERS):
        send(
            gathered[k].at[1 - role, here[a2], here[a1]],
            resid[k].at[role],
            *pair(own_sem, 0, k),
            (1 - role, dev),
        )
        keep(gathered[k].at[role, here[a2], here[a1]], resid[k].at[role], own_sem, 0, k)
    relay(1)
    for k in range(3):
        settle(meta[k].at[pl.ds(0, 3)], meta_sem.at[1, 1, k])
    tables(0)
    pick(0)
    tables(1)
    pick(1)
    expert_in(0)
    expert_out(0)
    expert_in(1)
    expert_out(1)
    merge(0)
    merge(1)
    fold(0)
    fold(1)

    for k in range(3):
        settle(pieces[k], r2_sem.at[1, 0, k])
        settle(resid[k], own_sem.at[1, 0, k])
        for c in range(2):
            total = resid[k][c].astype(F32)
            for n in range(4):
                total = total + pieces[k][c, n].astype(F32)
            begin = c * HALF + FIRSTS[k]
            out[:, begin : begin + SIZES[k]] = total.astype(BF)

    for k in range(3):
        settle(meta[k].at[0, pl.ds(0, 3)], meta_sem.at[0, 0, k])
        settle(meta[k].at[pl.ds(0, 3)], meta_sem.at[0, 1, k])
        settle(resid[k].at[0], own_sem.at[0, 0, k])
        for b in range(2):
            settle(gathered[k].at[b, 0, pl.ds(0, 3)], g1_sem.at[0, b, k])
            settle(gathered[k].at[b, pl.ds(0, 3)], g2_sem.at[0, b, k])
            settle(picked[k].at[b, pl.ds(0, 7)], ex_sem.at[0, b, k])
            settle(picked[k].at[b, pl.ds(0, 7)], back_sem.at[0, b, k])
            settle(partial[k].at[b, pl.ds(0, 3)], r1_sem.at[0, b, k])
            settle(summed[k].at[b, pl.ds(0, 3)], r2_sem.at[0, b, k])
        settle(resid[k].at[0], own_sem.at[0, 1, k])


def per_device(
    queries,
    keys_cache,
    values_cache,
    new_keys,
    new_values,
    lengths,
    norm_gain,
    expert_ids,
    route_weights,
    gate_weight,
    up_weight,
    down_weight,
):
    def buffers(*lead):
        return [pltpu.VMEM((*lead, size), BF) for size in SIZES]

    vmem = pl.BlockSpec(memory_space=pltpu.VMEM)
    hbm = pl.BlockSpec(memory_space=pl.ANY)
    mixed = pl.pallas_call(
        kernel,
        name="layer",
        out_shape=jax.ShapeDtypeStruct((TOK, WIDTH), BF),
        in_specs=[pl.BlockSpec(memory_space=pltpu.SMEM)] + [vmem] * 6 + [hbm] * 5,
        out_specs=vmem,
        scratch_shapes=[
            *buffers(2, 4, 4, TOK),
            *buffers(2, 8, 32),
            *buffers(2, 2, 4, 32),
            *buffers(2, 2, 4, 32),
            *buffers(2, 8, 32),
            *buffers(2, 4, 64),
            *buffers(2, 4, 64),
            *buffers(2, 4, TOK),
            *buffers(2, 4, TOK),
            *buffers(2, TOK),
            *[pltpu.VMEM((4, 4, 2 * TOK, EXPERTS), BF)] * 3,
            pltpu.VMEM((2 * TOK, LEN_PAD, HEAD), BF),
            pltpu.VMEM((2 * TOK, LEN_PAD, HEAD), BF),
            pltpu.VMEM((2 * TOK * HEADS, HEAD), F32),
            pltpu.VMEM((WIDTH, FF), BF),
            pltpu.VMEM((WIDTH, FF), BF),
            pltpu.VMEM((FF, WIDTH), BF),
            pltpu.VMEM((128, WIDTH), BF),
            pltpu.VMEM((128, FF), F32),
            pltpu.VMEM((128, FF), F32),
            pltpu.VMEM((3, 128, FF), BF),
            pltpu.VMEM((2, 3, 256, 256), BF),
            pltpu.VMEM((2, 3, 256, 256), BF),
            pltpu.SemaphoreType.DMA((2, 2)),
            pltpu.SemaphoreType.DMA((3,)),
            *[pltpu.SemaphoreType.DMA((2, 2, 3))] * 8,
        ],
        compiler_params=pltpu.CompilerParams(
            collective_id=0, has_side_effects=True, vmem_limit_bytes=VMEM_LIMIT
        ),
        cost_estimate=pl.CostEstimate(
            flops=6 * 256 * WIDTH * FF, bytes_accessed=22 * 2**20, transcendentals=0
        ),
    )(
        lengths,
        expert_ids.T,
        route_weights.T,
        norm_gain.reshape(1, WIDTH),
        queries,
        new_keys.reshape(2 * TOK, HEAD),
        new_values.reshape(2 * TOK, HEAD),
        keys_cache,
        values_cache,
        gate_weight,
        up_weight,
        down_weight,
    )
    return mixed.reshape(1, 1, TOK, WIDTH)


def solution(mesh):
    return jax.shard_map(
        per_device,
        mesh=mesh,
        in_specs=(
            P("dev", "role", None),
            P("dev", "role", None, None),
            P("dev", "role", None, None),
            P("dev", "role", None),
            P("dev", "role", None),
            P("dev"),
            P(),
            P("dev", None),
            P("dev", None),
            P(("role", "dev"), None, None),
            P(("role", "dev"), None, None),
            P(("role", "dev"), None, None),
        ),
        out_specs=P("dev", "role", None, None),
        check_vma=False,
    )
```

```python
import jax
import jax.numpy as jnp
from jax import lax
from jax.experimental import pallas as pl
from jax.experimental.pallas import tpu as pltpu
from jax.sharding import PartitionSpec as P

HEAD = 128
HEADS = 16
TOK = 16
LEN = 192
LEN_PAD = 208
HALF = 2048
WIDTH = 4096
FF = 768
EXPERTS = 128
STRIDES = (16, 4, 1)
ORDERS = ((1, 0, 2), (0, 2, 1), (2, 1, 0))
SIZES = (768, 640, 640)
FIRSTS = (0, 768, 1408)
CHUNKS = (((0, 384), (0, 384), (0, 256)), ((384, 384), (384, 256), (256, 384)))
DISPATCH = ((0, 1), (None,))
RETURN = ((None,), (0, 1))
MESH = pl.DeviceIdType.MESH
VMEM_LIMIT = 52 * 2**20
BF = jnp.bfloat16
F32 = jnp.float32


def rows_dot(a, b):
    return lax.dot_general(a, b, (((1,), (1,)), ((), ())), preferred_element_type=F32)


def dot(a, b):
    return jnp.dot(a, b, preferred_element_type=F32)


def iotas(rows, cols):
    shape = (rows, cols)
    return lax.broadcasted_iota(jnp.int32, shape, 0), lax.broadcasted_iota(jnp.int32, shape, 1)


def span(j, k):
    return (0, SIZES[k]) if j is None else CHUNKS[j][k]


def kernel(*refs):
    small_hbm = refs[:7]
    keys_hbm, values_hbm, gate_hbm, up_hbm, down_hbm, out = refs[7:13]
    lengths, ids, route, gain, queries, new_keys, new_values = small = refs[13:20]
    refs = list(refs[20:])

    def take(count):
        taken = refs[:count]
        del refs[:count]
        return taken

    gathered, picked, arrived, produced, returned, partial, parts, summed, pieces, resid, meta = (
        take(3) for _ in range(11)
    )
    (keys, values, heads, gate_w, up_w, down_w, normed, gate, up, hidden, squares) = take(11)
    select, combine = take(2)
    (small_sem, load_sem, weight_sem, meta_sem, g1_sem, g2_sem, ex_sem, back_sem, r1_sem, r2_sem, own_sem) = (
        take(11)
    )

    role = lax.axis_index("role")
    dev = lax.axis_index("dev")
    here = (dev // 16, (dev // 4) % 4, dev % 4)

    def at(axis, value):
        return dev + (value - here[axis]) * STRIDES[axis]

    def along(axis, step):
        return lax.rem(here[axis] + step, 4)

    def send(src, dst, send_sem, recv_sem, target):
        pltpu.make_async_remote_copy(
            src_ref=src,
            dst_ref=dst,
            send_sem=send_sem,
            recv_sem=recv_sem,
            device_id=target,
            device_id_type=MESH,
        ).start()

    def pair(sems, *index):
        return sems.at[0, *index], sems.at[1, *index]

    def keep(src, dst, sems, *index):
        pltpu.make_async_copy(src, dst, sems.at[1, *index]).start()

    def lanes(ref, j, k):
        first, size = span(j, k)
        return ref if j is None else ref.at[..., pl.ds(first, size)]

    def settle(ref, sem):
        pltpu.make_async_copy(ref, ref, sem).wait()

    small_loads = [
        pltpu.make_async_copy(src, dst, small_sem.at[n])
        for n, (src, dst) in enumerate(zip(small_hbm, small))
    ]
    loads = [
        pltpu.make_async_copy(
            src.at[pl.ds(n * 8, 8), 0], dst.at[pl.ds(n * 8, 8), pl.ds(0, LEN)], load_sem.at[n, m]
        )
        for n in range(4)
        for m, (src, dst) in enumerate(((keys_hbm, keys), (values_hbm, values)))
    ]
    for copy in small_loads[:3] + loads[:2] + small_loads[3:] + loads[2:]:
        copy.start()

    def load_weights():
        for n, (src, dst) in enumerate(((gate_hbm, gate_w), (up_hbm, up_w))):
            for j in range(2):
                place = j * HALF
                for c in range(2):
                    for k in range(3):
                        first, size = CHUNKS[j][k]
                        pltpu.make_async_copy(
                            src.at[0, pl.ds(c * HALF + FIRSTS[k] + first, size)],
                            dst.at[pl.ds(place, size)],
                            weight_sem.at[n, j],
                        ).start()
                        place += size
        pltpu.make_async_copy(down_hbm.at[0], down_w, weight_sem.at[2, 0]).start()

    barrier = pltpu.get_barrier_semaphore()
    for axis in range(3):
        for step in (1, 2, 3):
            for who in range(2):
                pl.semaphore_signal(
                    barrier, inc=1, device_id=(who, at(axis, along(axis, step))), device_id_type=MESH
                )
    pl.semaphore_signal(barrier, inc=1, device_id=(1 - role, dev), device_id_type=MESH)

    small_loads[1].wait()
    small_loads[2].wait()
    both = 2 * TOK
    row, col = iotas(EXPERTS, both)
    share = route[...] / jnp.sum(route[...], axis=0, keepdims=True)
    named = ids[...]
    hit = jnp.zeros((EXPERTS, both), F32)
    shares = jnp.zeros((EXPERTS, both), F32)
    for k in range(named.shape[0]):
        same = named[k : k + 1, :] == row
        hit = jnp.where(same, 1.0, hit)
        shares = jnp.where(same, share[k : k + 1, :], shares)
    row, col = iotas(both, both)
    before = jnp.where((row // TOK == col // TOK) & (row < col), 1.0, 0.0).astype(BF)
    second = dot(hit.astype(BF), before)
    signed = jnp.where(second > 0.5, -shares, shares).astype(BF)
    signed = rows_dot(jnp.where(row == col, 1.0, 0.0).astype(BF), signed).astype(BF)
    for k, (a1, a2, _) in enumerate(ORDERS):
        meta[k][here[a2], here[a1]] = signed

    scale = HEAD ** (-0.5)
    first_row = lax.broadcasted_iota(jnp.int32, (16, HEAD), 0) == 0
    place = lax.broadcasted_iota(jnp.int32, (HEADS, LEN_PAD), 1)

    def attend(first):
        scores = []
        for n in range(8):
            r = first + n
            own_key = jnp.broadcast_to(new_keys[pl.ds(r, 1), :], (16, HEAD)).astype(F32)
            own_value = jnp.broadcast_to(new_values[pl.ds(r, 1), :], (16, HEAD)).astype(F32)
            keys[r, LEN:LEN_PAD, :] = jnp.where(first_row, own_key, 0.0).astype(BF)
            values[r, LEN:LEN_PAD, :] = jnp.where(first_row, own_value, 0.0).astype(BF)
            live = (place < lengths[r]) | (place == LEN)
            scores.append(jnp.where(live, rows_dot(queries[r], keys[r]) * scale, -jnp.inf))
        scores = jnp.concatenate(scores, axis=0)
        spread = jnp.exp(scores - jnp.max(scores, axis=1, keepdims=True))
        spread = (spread / jnp.sum(spread, axis=1, keepdims=True)).astype(BF)
        for n in range(8):
            r = first + n
            heads[r * HEADS : (r + 1) * HEADS, :] = dot(
                spread[n * HEADS : (n + 1) * HEADS], values[r]
            )

    def attend_batch(b):
        for n in range(2 * b, 2 * b + 2):
            loads[2 * n].wait()
            loads[2 * n + 1].wait()
            attend(n * 8)

    def put(b, j):
        for k, (a1, a2, _) in enumerate(ORDERS):
            first, size = span(j, k)
            block = gathered[k].at[b, here[a2], here[a1]]
            for h in range(first // HEAD, (first + size) // HEAD):
                head = FIRSTS[k] // HEAD + h
                block[:, h * HEAD : (h + 1) * HEAD] = heads[
                    pl.ds(b * TOK * HEADS + head, TOK, stride=HEADS), :
                ].astype(BF)
            block = lanes(block, j, k)
            for step in (2, 1, 3):
                send(block, block, *pair(g1_sem, b, j or 0, k), (role, at(a1, along(a1, step))))

    def relay(b, j):
        for k, (a1, a2, _) in enumerate(ORDERS):
            settle(lanes(gathered[k].at[b, 0, pl.ds(0, 3)], j, k), g1_sem.at[1, b, j or 0, k])
            block = lanes(gathered[k].at[b, here[a2]], j, k)
            for step in (2, 1, 3):
                send(block, block, *pair(g2_sem, b, j or 0, k), (role, at(a2, along(a2, step))))

    def tables(b):
        row, col = iotas(256, EXPERTS)
        tall_row, tall_col = iotas(256, 256)
        for k, (_, _, a3) in enumerate(ORDERS):
            expert = ((row // 32) % 2) * 64 + at(a3, row // 64)
            chosen = jnp.where(expert == col, 1.0, 0.0).astype(BF)
            marks = meta[k][:, :, b * TOK : (b + 1) * TOK, :].reshape(256, EXPERTS)
            wide = rows_dot(chosen, marks)
            wide = jnp.where(tall_row % 2 == 0, wide, -wide)
            mask = ((tall_row % 32) // 2 == tall_col // TOK) & (wide > 0.0)
            select[b, k] = jnp.where(mask, 1.0, 0.0).astype(BF)
            tall = rows_dot(marks, chosen)
            tall = jnp.where(tall_col % 2 == 0, tall, -tall)
            mask = ((tall_col % 32) // 2 == tall_row // TOK) & (tall > 0.0)
            combine[b, k] = jnp.where(mask, tall, 0.0).astype(BF)

    def pick(b, j):
        for k, (_, _, a3) in enumerate(ORDERS):
            first, size = span(j, k)
            settle(lanes(gathered[k].at[b, pl.ds(0, 3)], j, k), g2_sem.at[1, b, j or 0, k])
            tokens = gathered[k][b, :, :, :, first : first + size].reshape(256, size)
            rows = dot(select[b, k], tokens).astype(BF)
            picked[k][b, :, :, first : first + size] = rows.reshape(8, 32, size)
            there = lanes(arrived[k].at[b, role, here[a3]], j, k)
            sems = pair(ex_sem, b, j or 0, k)
            for step in (2, 1, 3):
                z = along(a3, step)
                for who in range(2):
                    send(lanes(picked[k].at[b, z * 2 + who], j, k), there, *sems, (who, at(a3, z)))
            mine = here[a3] * 2
            send(lanes(picked[k].at[b, mine + 1 - role], j, k), there, *sems, (1 - role, dev))
            keep(lanes(picked[k].at[b, mine + role], j, k), there, ex_sem, b, j or 0, k)

    def turned(index, k):
        a1, a2, a3 = ORDERS[0]
        place = {a3: index // 32, a2: (index // 8) % 4, a1: (index // 2) % 4}
        a1, a2, a3 = ORDERS[k]
        return place[a3] * 32 + place[a2] * 8 + place[a1] * 2 + index % 2

    def expert_in(b, j):
        row, col = iotas(128, 128)
        chunks = (0, 1) if j is None else (j,)
        total = jnp.zeros((128, HEAD), F32) if 0 in chunks else squares[...]
        for k in range(3):
            settle(lanes(arrived[k].at[b], j, k), ex_sem.at[1, b, j or 0, k])
            for part in chunks:
                place = part * HALF + sum(size for _, size in CHUNKS[part][:k])
                for c in range(2):
                    first, size = CHUNKS[part][k]
                    rows = arrived[k][b, c, :, :, first : first + size].reshape(128, size)
                    if k == 0:
                        rows = rows.astype(F32)
                    else:
                        rows = dot(jnp.where(turned(row, k) == col, 1.0, 0.0).astype(BF), rows)
                    for t in range(size // HEAD):
                        tile = rows[:, t * HEAD : (t + 1) * HEAD]
                        total = total + tile * tile
                    begin = c * HALF + FIRSTS[k] + first
                    normed[:, place : place + size] = (rows * gain[:, begin : begin + size]).astype(BF)
                    place += 1024
        squares[...] = total
        if b == 0:
            for part in chunks:
                settle(gate_w.at[pl.ds(part * HALF, HALF)], weight_sem.at[0, part])
                settle(up_w.at[pl.ds(part * HALF, HALF)], weight_sem.at[1, part])
        begin, end = chunks[0] * HALF, (chunks[-1] + 1) * HALF

        def tile(n, carry):
            cols = pl.ds(pl.multiple_of(n * 256, 256), 256)
            for total, weight in ((gate, gate_w), (up, up_w)):
                product = dot(normed[:, begin:end], weight[begin:end, cols])
                total[:, cols] = product if 0 in chunks else total[:, cols] + product
            return carry

        lax.fori_loop(0, FF // 256, tile, 0)

    def expert_mid():
        row, col = iotas(128, 128)
        factor = lax.rsqrt(jnp.sum(squares[...], axis=1, keepdims=True) * (1.0 / WIDTH) + 1e-06)
        gated = gate[...] * factor
        hidden[0] = (gated / (1.0 + jnp.exp(-gated)) * (up[...] * factor)).astype(BF)
        for k in (1, 2):
            turn = jnp.where(turned(col, k) == row, 1.0, 0.0).astype(BF)
            hidden[k] = dot(turn, hidden[0]).astype(BF)

    def expert_out(b, j):
        if b == 0 and j != 1:
            settle(down_w, weight_sem.at[2, 0])
        for k, (_, _, a3) in enumerate(ORDERS):
            first, size = span(j, k)
            for c in range(2):
                begin = c * HALF + FIRSTS[k] + first
                rows = dot(hidden[k], down_w[:, begin : begin + size]).astype(BF)
                produced[k][b, c, :, :, first : first + size] = rows.reshape(4, 32, size)
            there = lanes(returned[k].at[b, here[a3] * 2 + role], j, k)
            sems = pair(back_sem, b, j or 0, k)
            for step in (2, 1, 3):
                z = along(a3, step)
                for who in range(2):
                    send(lanes(produced[k].at[b, who, z], j, k), there, *sems, (who, at(a3, z)))
            mine = produced[k].at[b, :, here[a3]]
            send(lanes(mine.at[1 - role], j, k), there, *sems, (1 - role, dev))
            keep(lanes(mine.at[role], j, k), there, back_sem, b, j or 0, k)

    def merge(b, j):
        for k, (_, a2, _) in enumerate(ORDERS):
            first, size = span(j, k)
            settle(lanes(returned[k].at[b], j, k), back_sem.at[1, b, j or 0, k])
            rows = returned[k][b, :, :, first : first + size].reshape(256, size)
            rows = dot(combine[b, k], rows).astype(BF)
            partial[k][b, :, :, first : first + size] = rows.reshape(4, 64, size)
            there = lanes(parts[k].at[b, here[a2]], j, k)
            for step in (2, 1, 3):
                z = along(a2, step)
                send(
                    lanes(partial[k].at[b, z], j, k),
                    there,
                    *pair(r1_sem, b, j or 0, k),
                    (role, at(a2, z)),
                )
            keep(lanes(partial[k].at[b, here[a2]], j, k), there, r1_sem, b, j or 0, k)

    def fold(b, j):
        for k, (a1, _, _) in enumerate(ORDERS):
            first, size = span(j, k)
            settle(lanes(parts[k].at[b], j, k), r1_sem.at[1, b, j or 0, k])
            total = parts[k][b, 0, :, first : first + size].astype(F32)
            for n in range(1, 4):
                total = total + parts[k][b, n, :, first : first + size].astype(F32)
            summed[k][b, :, :, first : first + size] = total.astype(BF).reshape(4, TOK, size)
            there = lanes(pieces[k].at[role, here[a1]], j, k)
            arrival = r2_sem.at[1, 0, 0, k]
            for step in (2, 1, 3):
                z = along(a1, step)
                send(
                    lanes(summed[k].at[b, z], j, k),
                    there,
                    r2_sem.at[0, b, j or 0, k],
                    arrival,
                    (b, at(a1, z)),
                )
            mine = lanes(summed[k].at[b, here[a1]], j, k)

            @pl.when(role == b)
            def _(mine=mine, there=there, arrival=arrival):
                pltpu.make_async_copy(mine, there, arrival).start()

            @pl.when(role != b)
            def _(mine=mine, there=there, arrival=arrival, k=k):
                send(mine, there, own_sem.at[0, 1, j or 0, k], arrival, (b, dev))

    def left_dispatch():
        for k in range(3):
            settle(meta[k].at[0, pl.ds(0, 3)], meta_sem.at[0, 0, 0, k])
            settle(meta[k].at[pl.ds(0, 3)], meta_sem.at[0, 1, 0, k])
            settle(resid[k].at[0], own_sem.at[0, 0, 0, k])
            for b in range(2):
                for j in DISPATCH[b]:
                    block = lanes(gathered[k].at[b], j, k)
                    settle(block.at[0, pl.ds(0, 3)], g1_sem.at[0, b, j or 0, k])
                    settle(block.at[pl.ds(0, 3)], g2_sem.at[0, b, j or 0, k])
                    settle(lanes(picked[k].at[b, pl.ds(0, 7)], j, k), ex_sem.at[0, b, j or 0, k])

    def left_return(buffers, sems, blocks):
        for k in range(3):
            for b in range(2):
                for j in RETURN[b]:
                    block = lanes(buffers[k].at[b, pl.ds(0, blocks)], j, k)
                    settle(block, sems.at[0, b, j or 0, k])

    pl.semaphore_wait(barrier, 19)
    for k, (a1, a2, _) in enumerate(ORDERS):
        block = meta[k].at[here[a2], here[a1]]
        for step in (2, 1, 3):
            send(block, block, *pair(meta_sem, 0, 0, k), (role, at(a1, along(a1, step))))
    for n in (0, 3, 4, 5, 6):
        small_loads[n].wait()
    attend_batch(0)
    for j in DISPATCH[0]:
        put(0, j)
    attend_batch(1)
    for j in DISPATCH[1]:
        put(1, j)
    load_weights()
    for k, (a1, a2, _) in enumerate(ORDERS):
        settle(meta[k].at[0, pl.ds(0, 3)], meta_sem.at[1, 0, 0, k])
        block = meta[k].at[here[a2]]
        for step in (2, 1, 3):
            send(block, block, *pair(meta_sem, 1, 0, k), (role, at(a2, along(a2, step))))
    for j in DISPATCH[0]:
        relay(0, j)
    for k, (a1, a2, _) in enumerate(ORDERS):
        send(
            gathered[k].at[1 - role, here[a2], here[a1]],
            resid[k].at[role],
            *pair(own_sem, 0, 0, k),
            (1 - role, dev),
        )
        keep(gathered[k].at[role, here[a2], here[a1]], resid[k].at[role], own_sem, 0, 0, k)
    for j in DISPATCH[1]:
        relay(1, j)
    for k in range(3):
        settle(meta[k].at[pl.ds(0, 3)], meta_sem.at[1, 1, 0, k])
    tables(0)
    pick(0, 0)
    pick(0, 1)
    tables(1)
    pick(1, None)
    expert_in(0, 0)
    expert_in(0, 1)
    expert_mid()
    expert_out(0, None)
    expert_in(1, None)
    expert_mid()
    expert_out(1, 0)
    expert_out(1, 1)
    left_dispatch()
    merge(0, None)
    merge(1, 0)
    merge(1, 1)
    left_return(picked, back_sem, 7)
    fold(0, None)
    fold(1, 0)
    fold(1, 1)
    left_return(partial, r1_sem, 3)
    for k in range(3):
        settle(pieces[k], r2_sem.at[1, 0, 0, k])
        settle(resid[k], own_sem.at[1, 0, 0, k])
        for c in range(2):
            total = resid[k][c].astype(F32)
            for n in range(4):
                total = total + pieces[k][c, n].astype(F32)
            begin = c * HALF + FIRSTS[k]
            out[:, begin : begin + SIZES[k]] = total.astype(BF)

    for k in range(3):
        for b in range(2):
            for j in RETURN[b]:
                settle(lanes(summed[k].at[b, pl.ds(0, 3)], j, k), r2_sem.at[0, b, j or 0, k])

                @pl.when(role != b)
                def _(j=j, k=k):
                    settle(lanes(resid[k].at[0], j, k), own_sem.at[0, 1, j or 0, k])


def per_device(
    queries,
    keys_cache,
    values_cache,
    new_keys,
    new_values,
    lengths,
    norm_gain,
    expert_ids,
    route_weights,
    gate_weight,
    up_weight,
    down_weight,
):
    def buffers(*lead):
        return [pltpu.VMEM((*lead, size), BF) for size in SIZES]

    operands = (
        lengths,
        expert_ids.T,
        route_weights.T,
        norm_gain.reshape(1, WIDTH),
        queries,
        new_keys.reshape(2 * TOK, HEAD),
        new_values.reshape(2 * TOK, HEAD),
        keys_cache,
        values_cache,
        gate_weight,
        up_weight,
        down_weight,
    )
    hbm = pl.BlockSpec(memory_space=pltpu.HBM)
    mixed = pl.pallas_call(
        kernel,
        name="layer",
        out_shape=jax.ShapeDtypeStruct((TOK, WIDTH), BF),
        in_specs=[hbm] * 12,
        out_specs=pl.BlockSpec(memory_space=pltpu.VMEM),
        scratch_shapes=[
            pltpu.SMEM((2 * TOK,), jnp.int32),
            pltpu.VMEM((8, 2 * TOK), jnp.int32),
            pltpu.VMEM((8, 2 * TOK), F32),
            pltpu.VMEM((1, WIDTH), F32),
            pltpu.VMEM((2 * TOK, HEADS, HEAD), BF),
            pltpu.VMEM((2 * TOK, HEAD), BF),
            pltpu.VMEM((2 * TOK, HEAD), BF),
            *buffers(2, 4, 4, TOK),
            *buffers(2, 8, 32),
            *buffers(2, 2, 4, 32),
            *buffers(2, 2, 4, 32),
            *buffers(2, 8, 32),
            *buffers(2, 4, 64),
            *buffers(2, 4, 64),
            *buffers(2, 4, TOK),
            *buffers(2, 4, TOK),
            *buffers(2, TOK),
            *[pltpu.VMEM((4, 4, 2 * TOK, EXPERTS), BF)] * 3,
            pltpu.VMEM((2 * TOK, LEN_PAD, HEAD), BF),
            pltpu.VMEM((2 * TOK, LEN_PAD, HEAD), BF),
            pltpu.VMEM((2 * TOK * HEADS, HEAD), F32),
            pltpu.VMEM((WIDTH, FF), BF),
            pltpu.VMEM((WIDTH, FF), BF),
            pltpu.VMEM((FF, WIDTH), BF),
            pltpu.VMEM((128, WIDTH), BF),
            pltpu.VMEM((128, FF), F32),
            pltpu.VMEM((128, FF), F32),
            pltpu.VMEM((3, 128, FF), BF),
            pltpu.VMEM((128, HEAD), F32),
            pltpu.VMEM((2, 3, 256, 256), BF),
            pltpu.VMEM((2, 3, 256, 256), BF),
            pltpu.SemaphoreType.DMA((7,)),
            pltpu.SemaphoreType.DMA((4, 2)),
            pltpu.SemaphoreType.DMA((3, 2)),
            *[pltpu.SemaphoreType.DMA((2, 2, 2, 3))] * 8,
        ],
        compiler_params=pltpu.CompilerParams(
            collective_id=0, has_side_effects=True, vmem_limit_bytes=VMEM_LIMIT
        ),
        cost_estimate=pl.CostEstimate(
            flops=6 * 256 * WIDTH * FF, bytes_accessed=22 * 2**20, transcendentals=0
        ),
    )(*(pltpu.with_memory_space_constraint(operand, pltpu.HBM) for operand in operands))
    return mixed.reshape(1, 1, TOK, WIDTH)


def solution(mesh):
    return jax.shard_map(
        per_device,
        mesh=mesh,
        in_specs=(
            P("dev", "role", None),
            P("dev", "role", None, None),
            P("dev", "role", None, None),
            P("dev", "role", None),
            P("dev", "role", None),
            P("dev"),
            P(),
            P("dev", None),
            P("dev", None),
            P(("role", "dev"), None, None),
            P(("role", "dev"), None, None),
            P(("role", "dev"), None, None),
        ),
        out_specs=P("dev", "role", None, None),
        check_vma=False,
    )
```

```python
import jax
import jax.numpy as jnp
from jax import lax
from jax.experimental import pallas as pl
from jax.experimental.pallas import tpu as pltpu
from jax.sharding import PartitionSpec as P

HEAD = 128
HEADS = 16
TOK = 16
LEN = 192
LEN_PAD = 208
HALF = 2048
WIDTH = 4096
FF = 768
EXPERTS = 128
STRIDES = (16, 4, 1)
ORDERS = ((1, 0, 2), (0, 2, 1), (2, 1, 0))
SIZES = (768, 640, 640)
FIRSTS = (0, 768, 1408)
CHUNKS = (((0, 384), (0, 384), (0, 256)), ((384, 384), (384, 256), (256, 384)))
DISPATCH = ((0, 1), (None,))
RETURN = ((None,), (0, 1))
MESH = pl.DeviceIdType.MESH
VMEM_LIMIT = 52 * 2**20
BF = jnp.bfloat16
F32 = jnp.float32


def rows_dot(a, b):
    return lax.dot_general(a, b, (((1,), (1,)), ((), ())), preferred_element_type=F32)


def dot(a, b):
    return jnp.dot(a, b, preferred_element_type=F32)


def iotas(rows, cols):
    shape = (rows, cols)
    return lax.broadcasted_iota(jnp.int32, shape, 0), lax.broadcasted_iota(jnp.int32, shape, 1)


def span(j, k):
    return (0, SIZES[k]) if j is None else CHUNKS[j][k]


def kernel(*refs):
    small_hbm = refs[:7]
    keys_hbm, values_hbm, gate_hbm, up_hbm, down_hbm, out = refs[7:13]
    lengths, ids, route, gain, queries, new_keys, new_values = small = refs[13:20]
    refs = list(refs[20:])

    def take(count):
        taken = refs[:count]
        del refs[:count]
        return taken

    gathered, picked, arrived, produced, returned, partial, parts, summed, pieces, resid, meta = (
        take(3) for _ in range(11)
    )
    brief, inbox = take(3), take(3)
    (keys, values, heads, gate_w, up_w, down_w, normed, gate, up, hidden, squares) = take(11)
    select, combine = take(2)
    (small_sem, load_sem, weight_sem, meta_sem, g1_sem, g2_sem, ex_sem, back_sem, r1_sem, r2_sem, own_sem) = (
        take(11)
    )

    role = lax.axis_index("role")
    dev = lax.axis_index("dev")
    here = (dev // 16, (dev // 4) % 4, dev % 4)

    def at(axis, value):
        return dev + (value - here[axis]) * STRIDES[axis]

    def along(axis, step):
        return lax.rem(here[axis] + step, 4)

    def send(src, dst, send_sem, recv_sem, target):
        pltpu.make_async_remote_copy(
            src_ref=src,
            dst_ref=dst,
            send_sem=send_sem,
            recv_sem=recv_sem,
            device_id=target,
            device_id_type=MESH,
        ).start()

    def pair(sems, *index):
        return sems.at[0, *index], sems.at[1, *index]

    def keep(src, dst, sems, *index):
        pltpu.make_async_copy(src, dst, sems.at[1, *index]).start()

    def lanes(ref, j, k):
        first, size = span(j, k)
        return ref if j is None else ref.at[..., pl.ds(first, size)]

    def settle(ref, sem):
        pltpu.make_async_copy(ref, ref, sem).wait()

    small_loads = [
        pltpu.make_async_copy(src, dst, small_sem.at[n])
        for n, (src, dst) in enumerate(zip(small_hbm, small))
    ]
    loads = [
        pltpu.make_async_copy(
            src.at[pl.ds(n * 8, 8), 0], dst.at[pl.ds(n * 8, 8), pl.ds(0, LEN)], load_sem.at[n, m]
        )
        for n in range(4)
        for m, (src, dst) in enumerate(((keys_hbm, keys), (values_hbm, values)))
    ]
    for copy in small_loads[1:3]:
        copy.start()

    def load_weights():
        for n, (src, dst) in enumerate(((gate_hbm, gate_w), (up_hbm, up_w))):
            for j in range(2):
                place = j * HALF
                for c in range(2):
                    for k in range(3):
                        first, size = CHUNKS[j][k]
                        pltpu.make_async_copy(
                            src.at[0, pl.ds(c * HALF + FIRSTS[k] + first, size)],
                            dst.at[pl.ds(place, size)],
                            weight_sem.at[n, j],
                        ).start()
                        place += size
        pltpu.make_async_copy(down_hbm.at[0], down_w, weight_sem.at[2, 0]).start()

    barrier = pltpu.get_barrier_semaphore()
    for axis in range(3):
        for step in (1, 2, 3):
            for who in range(2):
                pl.semaphore_signal(
                    barrier, inc=1, device_id=(who, at(axis, along(axis, step))), device_id_type=MESH
                )
    pl.semaphore_signal(barrier, inc=1, device_id=(1 - role, dev), device_id_type=MESH)

    for copy in small_loads[:1] + loads[:2] + small_loads[3:] + loads[2:]:
        copy.start()

    small_loads[1].wait()
    small_loads[2].wait()
    both = 2 * TOK
    row, col = iotas(EXPERTS, both)
    share = route[...] / jnp.sum(route[...], axis=0, keepdims=True)
    named = ids[...]
    hit = jnp.zeros((EXPERTS, both), F32)
    shares = jnp.zeros((EXPERTS, both), F32)
    for k in range(named.shape[0]):
        same = named[k : k + 1, :] == row
        hit = jnp.where(same, 1.0, hit)
        shares = jnp.where(same, share[k : k + 1, :], shares)
    row, col = iotas(both, both)
    before = jnp.where((row // TOK == col // TOK) & (row < col), 1.0, 0.0).astype(BF)
    second = dot(hit.astype(BF), before)
    signed = jnp.where(second > 0.5, -shares, shares).astype(BF)
    signed = rows_dot(jnp.where(row == col, 1.0, 0.0).astype(BF), signed).astype(BF)
    for k, (a1, a2, _) in enumerate(ORDERS):
        meta[k][here[a2], here[a1]] = signed

    scale = HEAD ** (-0.5)
    first_row = lax.broadcasted_iota(jnp.int32, (16, HEAD), 0) == 0
    place = lax.broadcasted_iota(jnp.int32, (HEADS, LEN_PAD), 1)

    def attend(first):
        scores = []
        for n in range(8):
            r = first + n
            own_key = jnp.broadcast_to(new_keys[pl.ds(r, 1), :], (16, HEAD)).astype(F32)
            own_value = jnp.broadcast_to(new_values[pl.ds(r, 1), :], (16, HEAD)).astype(F32)
            keys[r, LEN:LEN_PAD, :] = jnp.where(first_row, own_key, 0.0).astype(BF)
            values[r, LEN:LEN_PAD, :] = jnp.where(first_row, own_value, 0.0).astype(BF)
            live = (place < lengths[r]) | (place == LEN)
            scores.append(jnp.where(live, rows_dot(queries[r], keys[r]) * scale, -jnp.inf))
        scores = jnp.concatenate(scores, axis=0)
        spread = jnp.exp(scores - jnp.max(scores, axis=1, keepdims=True))
        spread = (spread / jnp.sum(spread, axis=1, keepdims=True)).astype(BF)
        for n in range(8):
            r = first + n
            heads[r * HEADS : (r + 1) * HEADS, :] = dot(
                spread[n * HEADS : (n + 1) * HEADS], values[r]
            )

    def attend_batch(b):
        for n in range(2 * b, 2 * b + 2):
            loads[2 * n].wait()
            loads[2 * n + 1].wait()
            attend(n * 8)

    def put(b, j):
        for k, (a1, a2, _) in enumerate(ORDERS):
            first, size = span(j, k)
            block = gathered[k].at[b, here[a2], here[a1]]
            for h in range(first // HEAD, (first + size) // HEAD):
                head = FIRSTS[k] // HEAD + h
                block[:, h * HEAD : (h + 1) * HEAD] = heads[
                    pl.ds(b * TOK * HEADS + head, TOK, stride=HEADS), :
                ].astype(BF)
            block = lanes(block, j, k)
            for step in (2, 1, 3):
                send(block, block, *pair(g1_sem, b, j or 0, k), (role, at(a1, along(a1, step))))

    def relay(b, j):
        for k, (a1, a2, _) in enumerate(ORDERS):
            settle(lanes(gathered[k].at[b, 0, pl.ds(0, 3)], j, k), g1_sem.at[1, b, j or 0, k])
            block = lanes(gathered[k].at[b, here[a2]], j, k)
            for step in (2, 1, 3):
                send(block, block, *pair(g2_sem, b, j or 0, k), (role, at(a2, along(a2, step))))

    def tables(b):
        row, col = iotas(256, 16)
        expand = jnp.where(row // 32 == col, 1.0, 0.0).astype(BF)
        row, col = iotas(128, 256)
        lane = jnp.where(row == (col % 64) // TOK * 2 * TOK + b * TOK + col % TOK, 1.0, 0.0)
        row, place = iotas(256, 256)
        for k in range(3):
            marks = jnp.zeros((16, 256), F32)
            for n in range(4):
                spread = jnp.where(col // 64 == n, lane, 0.0).astype(BF)
                marks = marks + dot(inbox[k][n], spread)
            wide = dot(expand, marks.astype(BF))
            wide = jnp.where(row % 2 == 0, wide, -wide)
            mask = ((row % 32) // 2 == place // TOK) & (wide > 0.0)
            select[b, k] = jnp.where(mask, 1.0, 0.0).astype(BF)
            combine[b, k] = jnp.where(mask, wide, 0.0).T.astype(BF)

    def pick(b, j):
        for k, (_, _, a3) in enumerate(ORDERS):
            first, size = span(j, k)
            settle(lanes(gathered[k].at[b, pl.ds(0, 3)], j, k), g2_sem.at[1, b, j or 0, k])
            tokens = gathered[k][b, :, :, :, first : first + size].reshape(256, size)
            rows = dot(select[b, k], tokens).astype(BF)
            picked[k][b, :, :, first : first + size] = rows.reshape(8, 32, size)
            there = lanes(arrived[k].at[b, role, here[a3]], j, k)
            sems = pair(ex_sem, b, j or 0, k)
            for step in (2, 1, 3):
                z = along(a3, step)
                for who in range(2):
                    send(lanes(picked[k].at[b, z * 2 + who], j, k), there, *sems, (who, at(a3, z)))
            mine = here[a3] * 2
            send(lanes(picked[k].at[b, mine + 1 - role], j, k), there, *sems, (1 - role, dev))
            keep(lanes(picked[k].at[b, mine + role], j, k), there, ex_sem, b, j or 0, k)

    def turned(index, k):
        a1, a2, a3 = ORDERS[0]
        place = {a3: index // 32, a2: (index // 8) % 4, a1: (index // 2) % 4}
        a1, a2, a3 = ORDERS[k]
        return place[a3] * 32 + place[a2] * 8 + place[a1] * 2 + index % 2

    def expert_in(b, j):
        row, col = iotas(128, 128)
        chunks = (0, 1) if j is None else (j,)
        total = jnp.zeros((128, HEAD), F32) if 0 in chunks else squares[...]
        for k in range(3):
            settle(lanes(arrived[k].at[b], j, k), ex_sem.at[1, b, j or 0, k])
            for part in chunks:
                place = part * HALF + sum(size for _, size in CHUNKS[part][:k])
                for c in range(2):
                    first, size = CHUNKS[part][k]
                    rows = arrived[k][b, c, :, :, first : first + size].reshape(128, size)
                    if k == 0:
                        rows = rows.astype(F32)
                    else:
                        rows = dot(jnp.where(turned(row, k) == col, 1.0, 0.0).astype(BF), rows)
                    for t in range(size // HEAD):
                        tile = rows[:, t * HEAD : (t + 1) * HEAD]
                        total = total + tile * tile
                    begin = c * HALF + FIRSTS[k] + first
                    normed[:, place : place + size] = (rows * gain[:, begin : begin + size]).astype(BF)
                    place += 1024
        squares[...] = total
        if b == 0:
            for part in chunks:
                settle(gate_w.at[pl.ds(part * HALF, HALF)], weight_sem.at[0, part])
                settle(up_w.at[pl.ds(part * HALF, HALF)], weight_sem.at[1, part])
        begin, end = chunks[0] * HALF, (chunks[-1] + 1) * HALF

        def tile(n):
            cols = pl.ds(n * 256, 256)
            for total, weight in ((gate, gate_w), (up, up_w)):
                product = dot(normed[:, begin:end], weight[begin:end, cols])
                total[:, cols] = product if 0 in chunks else total[:, cols] + product

        for n in range(FF // 256):
            tile(n)

    def expert_mid():
        row, col = iotas(128, 128)
        factor = lax.rsqrt(jnp.sum(squares[...], axis=1, keepdims=True) * (1.0 / WIDTH) + 1e-06)
        gated = gate[...] * factor
        hidden[0] = (gated / (1.0 + jnp.exp(-gated)) * (up[...] * factor)).astype(BF)
        for k in (1, 2):
            turn = jnp.where(turned(col, k) == row, 1.0, 0.0).astype(BF)
            hidden[k] = dot(turn, hidden[0]).astype(BF)

    def expert_out(b, j):
        if b == 0 and j != 1:
            settle(down_w, weight_sem.at[2, 0])
        for k, (_, _, a3) in enumerate(ORDERS):
            first, size = span(j, k)
            for c in range(2):
                begin = c * HALF + FIRSTS[k] + first
                rows = dot(hidden[k], down_w[:, begin : begin + size]).astype(BF)
                produced[k][b, c, :, :, first : first + size] = rows.reshape(4, 32, size)
            there = lanes(returned[k].at[b, here[a3] * 2 + role], j, k)
            sems = pair(back_sem, b, j or 0, k)
            for step in (2, 1, 3):
                z = along(a3, step)
                for who in range(2):
                    send(lanes(produced[k].at[b, who, z], j, k), there, *sems, (who, at(a3, z)))
            mine = produced[k].at[b, :, here[a3]]
            send(lanes(mine.at[1 - role], j, k), there, *sems, (1 - role, dev))
            keep(lanes(mine.at[role], j, k), there, back_sem, b, j or 0, k)

    def merge(b, j):
        for k, (_, a2, _) in enumerate(ORDERS):
            first, size = span(j, k)
            settle(lanes(returned[k].at[b], j, k), back_sem.at[1, b, j or 0, k])
            rows = returned[k][b, :, :, first : first + size].reshape(256, size)
            rows = dot(combine[b, k], rows).astype(BF)
            partial[k][b, :, :, first : first + size] = rows.reshape(4, 64, size)
            there = lanes(parts[k].at[b, here[a2]], j, k)
            for step in (2, 1, 3):
                z = along(a2, step)
                send(
                    lanes(partial[k].at[b, z], j, k),
                    there,
                    *pair(r1_sem, b, j or 0, k),
                    (role, at(a2, z)),
                )
            keep(lanes(partial[k].at[b, here[a2]], j, k), there, r1_sem, b, j or 0, k)

    def fold(b, j):
        for k, (a1, _, _) in enumerate(ORDERS):
            first, size = span(j, k)
            settle(lanes(parts[k].at[b], j, k), r1_sem.at[1, b, j or 0, k])
            total = parts[k][b, 0, :, first : first + size].astype(F32)
            for n in range(1, 4):
                total = total + parts[k][b, n, :, first : first + size].astype(F32)
            summed[k][b, :, :, first : first + size] = total.astype(BF).reshape(4, TOK, size)
            there = lanes(pieces[k].at[role, here[a1]], j, k)
            arrival = r2_sem.at[1, 0, 0, k]
            for step in (2, 1, 3):
                z = along(a1, step)
                send(
                    lanes(summed[k].at[b, z], j, k),
                    there,
                    r2_sem.at[0, b, j or 0, k],
                    arrival,
                    (b, at(a1, z)),
                )
            mine = lanes(summed[k].at[b, here[a1]], j, k)

            @pl.when(role == b)
            def _(mine=mine, there=there, arrival=arrival):
                pltpu.make_async_copy(mine, there, arrival).start()

            @pl.when(role != b)
            def _(mine=mine, there=there, arrival=arrival, k=k):
                send(mine, there, own_sem.at[0, 1, j or 0, k], arrival, (b, dev))

    def left_dispatch():
        for k in range(3):
            settle(meta[k].at[0, pl.ds(0, 3)], meta_sem.at[0, 0, 0, k])
            settle(inbox[k].at[pl.ds(0, 3)], meta_sem.at[0, 1, 0, k])
            settle(resid[k].at[0], own_sem.at[0, 0, 0, k])
            for b in range(2):
                for j in DISPATCH[b]:
                    block = lanes(gathered[k].at[b], j, k)
                    settle(block.at[0, pl.ds(0, 3)], g1_sem.at[0, b, j or 0, k])
                    settle(block.at[pl.ds(0, 3)], g2_sem.at[0, b, j or 0, k])
                    settle(lanes(picked[k].at[b, pl.ds(0, 7)], j, k), ex_sem.at[0, b, j or 0, k])

    def left_return(buffers, sems, blocks):
        for k in range(3):
            for b in range(2):
                for j in RETURN[b]:
                    block = lanes(buffers[k].at[b, pl.ds(0, blocks)], j, k)
                    settle(block, sems.at[0, b, j or 0, k])

    pl.semaphore_wait(barrier, 19)
    for k, (a1, a2, _) in enumerate(ORDERS):
        block = meta[k].at[here[a2], here[a1]]
        for step in (2, 1, 3):
            send(block, block, *pair(meta_sem, 0, 0, k), (role, at(a1, along(a1, step))))
    for n in (0, 3, 4, 5, 6):
        small_loads[n].wait()
    attend_batch(0)
    for j in DISPATCH[0]:
        put(0, j)
    attend_batch(1)
    for j in DISPATCH[1]:
        put(1, j)
    load_weights()
    row, col = iotas(64, EXPERTS)
    for k, (a1, a2, a3) in enumerate(ORDERS):
        settle(meta[k].at[0, pl.ds(0, 3)], meta_sem.at[1, 0, 0, k])
        shift = (row // 16 - here[a2]) * STRIDES[a2] + ((row // 2) % 4 - here[a3]) * STRIDES[a3]
        wanted = jnp.where((row % 2) * 64 + dev + shift == col, 1.0, 0.0).astype(BF)
        shares = rows_dot(wanted, meta[k][here[a2]].reshape(128, EXPERTS))
        brief[k][...] = shares.astype(BF).reshape(4, 16, 128)
        inbox[k][here[a2]] = brief[k][here[a2]]
        for step in (2, 1, 3):
            there = along(a2, step)
            send(
                brief[k].at[there],
                inbox[k].at[here[a2]],
                *pair(meta_sem, 1, 0, k),
                (role, at(a2, there)),
            )
    for j in DISPATCH[0]:
        relay(0, j)
    for k, (a1, a2, _) in enumerate(ORDERS):
        send(
            gathered[k].at[1 - role, here[a2], here[a1]],
            resid[k].at[role],
            *pair(own_sem, 0, 0, k),
            (1 - role, dev),
        )
        keep(gathered[k].at[role, here[a2], here[a1]], resid[k].at[role], own_sem, 0, 0, k)
    for j in DISPATCH[1]:
        relay(1, j)
    for k in range(3):
        settle(inbox[k].at[pl.ds(0, 3)], meta_sem.at[1, 1, 0, k])
    tables(0)
    pick(0, 0)
    pick(0, 1)
    tables(1)
    pick(1, None)
    expert_in(0, 0)
    expert_in(0, 1)
    expert_mid()
    expert_out(0, None)
    expert_in(1, None)
    expert_mid()
    expert_out(1, 0)
    expert_out(1, 1)
    left_dispatch()
    merge(0, None)
    merge(1, 0)
    merge(1, 1)
    left_return(picked, back_sem, 7)
    fold(0, None)
    fold(1, 0)
    fold(1, 1)
    left_return(partial, r1_sem, 3)
    for k in range(3):
        settle(pieces[k], r2_sem.at[1, 0, 0, k])
        settle(resid[k], own_sem.at[1, 0, 0, k])
        for c in range(2):
            total = resid[k][c].astype(F32)
            for n in range(4):
                total = total + pieces[k][c, n].astype(F32)
            begin = c * HALF + FIRSTS[k]
            out[:, begin : begin + SIZES[k]] = total.astype(BF)

    for k in range(3):
        for b in range(2):
            for j in RETURN[b]:
                settle(lanes(summed[k].at[b, pl.ds(0, 3)], j, k), r2_sem.at[0, b, j or 0, k])

                @pl.when(role != b)
                def _(j=j, k=k):
                    settle(lanes(resid[k].at[0], j, k), own_sem.at[0, 1, j or 0, k])


def per_device(
    queries,
    keys_cache,
    values_cache,
    new_keys,
    new_values,
    lengths,
    norm_gain,
    expert_ids,
    route_weights,
    gate_weight,
    up_weight,
    down_weight,
):
    def buffers(*lead):
        return [pltpu.VMEM((*lead, size), BF) for size in SIZES]

    operands = (
        lengths,
        expert_ids.T,
        route_weights.T,
        norm_gain.reshape(1, WIDTH),
        queries,
        new_keys.reshape(2 * TOK, HEAD),
        new_values.reshape(2 * TOK, HEAD),
        keys_cache,
        values_cache,
        gate_weight,
        up_weight,
        down_weight,
    )
    hbm = pl.BlockSpec(memory_space=pltpu.HBM)
    mixed = pl.pallas_call(
        kernel,
        name="layer",
        out_shape=jax.ShapeDtypeStruct((TOK, WIDTH), BF),
        in_specs=[hbm] * 12,
        out_specs=pl.BlockSpec(memory_space=pltpu.VMEM),
        scratch_shapes=[
            pltpu.SMEM((2 * TOK,), jnp.int32),
            pltpu.VMEM((8, 2 * TOK), jnp.int32),
            pltpu.VMEM((8, 2 * TOK), F32),
            pltpu.VMEM((1, WIDTH), F32),
            pltpu.VMEM((2 * TOK, HEADS, HEAD), BF),
            pltpu.VMEM((2 * TOK, HEAD), BF),
            pltpu.VMEM((2 * TOK, HEAD), BF),
            *buffers(2, 4, 4, TOK),
            *buffers(2, 8, 32),
            *buffers(2, 2, 4, 32),
            *buffers(2, 2, 4, 32),
            *buffers(2, 8, 32),
            *buffers(2, 4, 64),
            *buffers(2, 4, 64),
            *buffers(2, 4, TOK),
            *buffers(2, 4, TOK),
            *buffers(2, TOK),
            *[pltpu.VMEM((4, 4, 2 * TOK, EXPERTS), BF)] * 3,
            *[pltpu.VMEM((4, 16, 128), BF)] * 6,
            pltpu.VMEM((2 * TOK, LEN_PAD, HEAD), BF),
            pltpu.VMEM((2 * TOK, LEN_PAD, HEAD), BF),
            pltpu.VMEM((2 * TOK * HEADS, HEAD), F32),
            pltpu.VMEM((WIDTH, FF), BF),
            pltpu.VMEM((WIDTH, FF), BF),
            pltpu.VMEM((FF, WIDTH), BF),
            pltpu.VMEM((128, WIDTH), BF),
            pltpu.VMEM((128, FF), F32),
            pltpu.VMEM((128, FF), F32),
            pltpu.VMEM((3, 128, FF), BF),
            pltpu.VMEM((128, HEAD), F32),
            pltpu.VMEM((2, 3, 256, 256), BF),
            pltpu.VMEM((2, 3, 256, 256), BF),
            pltpu.SemaphoreType.DMA((7,)),
            pltpu.SemaphoreType.DMA((4, 2)),
            pltpu.SemaphoreType.DMA((3, 2)),
            *[pltpu.SemaphoreType.DMA((2, 2, 2, 3))] * 8,
        ],
        compiler_params=pltpu.CompilerParams(
            collective_id=0, has_side_effects=True, vmem_limit_bytes=VMEM_LIMIT
        ),
        cost_estimate=pl.CostEstimate(
            flops=6 * 256 * WIDTH * FF, bytes_accessed=22 * 2**20, transcendentals=0
        ),
    )(*(pltpu.with_memory_space_constraint(operand, pltpu.HBM) for operand in operands))
    return mixed.reshape(1, 1, TOK, WIDTH)


def solution(mesh):
    return jax.shard_map(
        per_device,
        mesh=mesh,
        in_specs=(
            P("dev", "role", None),
            P("dev", "role", None, None),
            P("dev", "role", None, None),
            P("dev", "role", None),
            P("dev", "role", None),
            P("dev"),
            P(),
            P("dev", None),
            P("dev", None),
            P(("role", "dev"), None, None),
            P(("role", "dev"), None, None),
            P(("role", "dev"), None, None),
        ),
        out_specs=P("dev", "role", None, None),
        check_vma=False,
    )
```
